512 devices in a mesh: seq: 128 (over z, x, core), grp: 4 (over y).
Axes of the slice: x: 4, y: 4, z: 16, core: 2. Of those that a mesh axis runs over, the one named last changes fastest.
Arguments:
- main_qkv: bfloat16 [49152, 3, 2560], P(('seq', 'grp')), may hold values from -6 to 6
- guide_qkv: bfloat16 [49152, 3, 768], P(('seq', 'grp')), may hold values from -6 to 6
- main_head: bfloat16 [2560, 64], P('grp'), may hold values from -2 to 2
- guide_head: bfloat16 [768, 64], replicated, may hold values from -3.5 to 3.5
- window_start: int32 [128], replicated, may hold values from 0 to 126, as said below
- timestep: int32 [1], replicated, may hold values from 0 to 999
Outputs:
- guided: float32 [49152, 64], P(('seq', 'grp'))
The draws below stay inside these ranges and needn't reach their ends.
Inputs may be any that keep to these rules, and one draw needn't show every extreme that they name: window_start[t] is t - 1 or t, drawn for each tile.
All inputs are finite; a program needn't handle non-finite values.
Results may differ from the reference program's by a relative error of at most 0.0041.
Values may be sent and summed in bfloat16 or wider, within the bound.
No kernel may reach another device: no remote copies, remote signals or barrier semaphores. Data moves between devices by JAX's collectives and lax.ppermute only.
A program may use at most 64 MiB of HBM per device.

```python
import math
import jax
import jax.numpy as jnp
from jax import lax

D = 2560
HEADS = 20
DG = 768
GHEADS = 6
HD = 128
TILE = 384
OUTC = 64
TILES = 128
TOKENS = 49152


def drawn_inputs(key, width):
    values = jax.random.normal(key, (TOKENS, 3, width), jnp.float32)
    return jnp.clip(values, -6.0, 6.0).astype(jnp.bfloat16)


def draw_main_qkv(key, part):
    key = jax.random.fold_in(key, 11)
    return drawn_inputs(key, D)


def draw_guide_qkv(key, part):
    key = jax.random.fold_in(key, 23)
    return drawn_inputs(key, DG)


def draw_window_start(key, part):
    key = jax.random.fold_in(key, 5)
    positions = jnp.arange(TILES, dtype=jnp.int32)
    backward = jax.random.randint(key, (TILES,), 0, 2, dtype=jnp.int32)
    return jnp.clip(positions - backward, 0, TILES - 2).astype(jnp.int32)


def steps_of(key, shape, shards, low, high):
    def one(axis_at, shards_of):
        heights = jax.random.uniform(jax.random.fold_in(jax.random.fold_in(key, 6), axis_at), (shards_of,), jnp.float32, low / len(shards), high / len(shards))
        return jnp.repeat(jnp.exp(heights), shape[axis_at] // shards_of).reshape((-1,) + (1,) * (len(shape) - axis_at - 1))

    factor_of = one(*shards[0])
    for cut in shards[1:]:
        factor_of = factor_of * one(*cut)
    return factor_of


def normal_values(rng, dims, deviation, bound, cuts=(), kind=jnp.bfloat16):
    factor_of = steps_of(rng, dims, cuts, -0.22, 0.18) if cuts else 1.0
    drawn = jax.random.normal(rng, dims, jnp.float32) * deviation * factor_of
    return jnp.minimum(jnp.maximum(drawn, -bound), bound).astype(kind)


def setup_inputs(seed: int = 0) -> dict:
    key_of = jax.random.split(jax.random.key(seed), 7)
    main_qkv = draw_main_qkv(jax.random.fold_in(key_of[6], 71), 0)
    guide_qkv = draw_guide_qkv(jax.random.fold_in(key_of[6], 71), 0)
    main_head = normal_values(key_of[2], (D, OUTC), (max(D // 256, 1)) ** -0.5, 2.0, ((0, 4),))
    guide_head = normal_values(key_of[3], (DG, OUTC), (max(DG // 256, 1)) ** -0.5, 3.5)
    window_start = draw_window_start(jax.random.fold_in(key_of[6], 71), 0)
    timestep = jax.random.randint(key_of[5], (1,), 0, 1000).astype(jnp.int32)
    return dict(main_qkv=main_qkv, guide_qkv=guide_qkv, main_head=main_head, guide_head=guide_head, window_start=window_start, timestep=timestep)


def head_attention(query, key_rows, value_rows, heads):
    q_count = query.shape[0]
    k_count = key_rows.shape[0]
    q_heads = query.reshape(q_count, heads, HD).astype(jnp.float32)
    k_heads = key_rows.reshape(k_count, heads, HD).astype(jnp.float32)
    v_heads = value_rows.reshape(k_count, heads, HD).astype(jnp.float32)
    scores = jnp.einsum('qhd,khd->hqk', q_heads, k_heads) * (1.0 / math.sqrt(HD))
    row_max = lax.optimization_barrier(jnp.max(scores, axis=-1, keepdims=True))
    lifted = jnp.exp(scores - row_max)
    row_sum = lax.optimization_barrier(jnp.sum(lifted, axis=-1, keepdims=True))
    weights = (lifted / row_sum).astype(jnp.bfloat16)
    weights = lax.optimization_barrier(weights).astype(jnp.float32)
    blended = jnp.einsum('hqk,khd->qhd', weights, v_heads)
    return blended.reshape(q_count, heads * HD).astype(jnp.bfloat16)

def reference(main_qkv, guide_qkv, main_head, guide_head, window_start, timestep):

    def one_tile(tile_pos):
        window_pos = window_start[tile_pos].astype(jnp.int32)
        main_rows = lax.dynamic_slice_in_dim(main_qkv, tile_pos * TILE, TILE, 0)
        main_window = lax.dynamic_slice_in_dim(main_qkv, window_pos * TILE, 2 * TILE, 0)
        main_mixed = head_attention(main_rows[:, 0], main_window[:, 1], main_window[:, 2], HEADS)
        guide_rows = lax.dynamic_slice_in_dim(guide_qkv, tile_pos * TILE, TILE, 0)
        guide_window = lax.dynamic_slice_in_dim(guide_qkv, window_pos * TILE, 2 * TILE, 0)
        guide_mixed = head_attention(guide_rows[:, 0], guide_window[:, 1], guide_window[:, 2], GHEADS)
        main_speed = jnp.dot(main_mixed, main_head, preferred_element_type=jnp.float32)
        guide_speed = jnp.dot(guide_mixed, guide_head, preferred_element_type=jnp.float32)
        return (main_speed, guide_speed)
    main_speed, guide_speed = lax.map(one_tile, jnp.arange(TILES, dtype=jnp.int32))
    main_speed = main_speed.reshape(TOKENS, OUTC)
    guide_speed = guide_speed.reshape(TOKENS, OUTC)
    weight = 1.0 + 2.0 * timestep[0].astype(jnp.float32) / 999.0
    return guide_speed + weight * (main_speed - guide_speed)
```

```python
import functools
import math

import jax
import jax.numpy as jnp
from jax import lax
from jax.experimental import pallas as pl
from jax.experimental.pallas import tpu as pltpu
from jax.sharding import PartitionSpec as P

HD = 128
TILE = 384
FIRST = 3
SCALE = 1.0 / math.sqrt(HD)
LIMIT = 24 * 1024 * 1024


def passed_along(block, axis, distance):
    devices = range(lax.axis_size(axis))
    route = [(i - distance, i) for i in devices if i - distance in devices]
    return lax.ppermute(block, axis, route)


def swapped(block):
    return lax.all_to_all(block, "grp", 0, 0)


def guide_pair(dst):
    return ((0, 1), (2, 1), (3, 4), (5, 4))[dst]


def pack(sources, groups, plan, rows):
    slabs = sorted({block[:2] for block in plan})

    def kernel(*refs):
        ins, out = refs[: len(sources)], refs[len(sources)]
        held, sem = refs[len(sources) + 1 : -1], refs[-1]
        copies = [
            pltpu.make_async_copy(ins[src].at[index], held[i], sem.at[i])
            for i, (src, index) in enumerate(slabs)
        ]
        for copy in copies:
            copy.start()
        for i, slab in enumerate(slabs):
            copies[i].wait()
            for src, index, row, count, head, group, at in plan:
                if (src, index) == slab:
                    out[group, pl.ds(at, count), :] = held[i][pl.ds(row, count), pl.ds(head * HD, HD)]

    return pl.pallas_call(
        kernel,
        out_shape=jax.ShapeDtypeStruct((groups, rows, HD), jnp.bfloat16),
        in_specs=[pl.BlockSpec(memory_space=pl.ANY)] * len(sources),
        out_specs=pl.BlockSpec(memory_space=pltpu.VMEM),
        scratch_shapes=[pltpu.VMEM(sources[src].shape[1:], jnp.bfloat16) for src, _ in slabs]
        + [pltpu.SemaphoreType.DMA((len(slabs),))],
        compiler_params=pltpu.CompilerParams(vmem_limit_bytes=LIMIT),
    )(*sources)


def head_mix(query, keys, values):
    scores = lax.dot_general(
        query, keys, (((1,), (1,)), ((), ())), preferred_element_type=jnp.float32
    )
    top = jnp.max(scores, axis=-1, keepdims=True)
    lifted = jnp.exp((scores - top) * SCALE)
    total = jnp.sum(lifted, axis=-1, keepdims=True)
    weights = (lifted * (1.0 / total)).astype(jnp.bfloat16)
    mixed = lax.dot_general(
        weights, values, (((1,), (0,)), ((), ())), preferred_element_type=jnp.float32
    )
    return mixed.astype(jnp.bfloat16)


def attention(side, half, weight, own, before, after, queries, main_head, guide_heads, earlier,
              heads, first_head, has_guide, tok):
    groups, rows, _ = own.shape
    q_rows = queries.shape[1]

    def kernel(side_ref, half_ref, weight_ref, own_ref, before_ref, after_ref, q_ref, wm_ref, wg_ref, earlier_ref,
               out_ref, kv, q_buf, mixed, sem):
        own_copy = pltpu.make_async_copy(own_ref, kv.at[0], sem.at[0])
        q_copy = pltpu.make_async_copy(q_ref, q_buf, sem.at[1])
        own_copy.start()
        q_copy.start()

        @pl.when(side_ref[0] == 0)
        def _():
            copy = pltpu.make_async_copy(before_ref, kv.at[1], sem.at[2])
            copy.start()
            copy.wait()

        @pl.when(side_ref[0] != 0)
        def _():
            copy = pltpu.make_async_copy(after_ref, kv.at[1], sem.at[2])
            copy.start()
            copy.wait()

        own_copy.wait()
        q_copy.wait()

        def window(block):
            return kv[:, :, pl.ds(block * tok, tok), :].reshape(2 * groups * tok, HD)

        for h in range(heads):
            query = q_buf[:, pl.ds((first_head + h) * tok, tok), :].reshape(groups * tok, HD)
            mixed[:, pl.ds(h * HD, HD)] = head_mix(query, window(2 * h), window(2 * h + 1))
        w = weight_ref[0]
        if has_guide:
            base = 2 * heads
            q_at = q_rows - tok - tok // 2
            query = q_buf[:, pl.ds(q_at, tok), :].reshape(groups * tok, HD)
            whole = head_mix(query, window(base), window(base + 1))
            query = q_buf[:, pl.ds(q_at + tok, tok // 2), :].reshape(groups * tok // 2, HD)
            shared = head_mix(query, window(base + 2), window(base + 3))
            shared = shared.reshape(groups, tok // 2, HD)
            blank = jnp.zeros_like(shared)
            upper = half_ref[0] != 0
            shared = jnp.concatenate(
                [jnp.where(upper, blank, shared), jnp.where(upper, shared, blank)], axis=1
            )
            whole = whole.reshape(groups, tok, HD)
        for j in range(groups):
            part = lax.dot_general(
                wm_ref[:, pl.ds(first_head * HD, heads * HD)], mixed[pl.ds(j * tok, tok), :],
                (((1,), (1,)), ((), ())), preferred_element_type=jnp.float32,
            ) * w
            if has_guide:
                side_by_side = jnp.concatenate([whole[j], shared[j]], axis=1)
                part += lax.dot_general(
                    wg_ref[...], side_by_side, (((1,), (1,)), ((), ())),
                    preferred_element_type=jnp.float32,
                ) * (1.0 - w)
                part += earlier_ref[j]
            out_ref[j] = part

    smem = pl.BlockSpec(memory_space=pltpu.SMEM)
    vmem = pl.BlockSpec(memory_space=pltpu.VMEM)
    anywhere = pl.BlockSpec(memory_space=pl.ANY)
    outc = main_head.shape[0]
    pairs = heads + (1.5 if has_guide else 0)
    flops = int(4 * pairs * groups * tok * 2 * groups * tok * HD)
    return pl.pallas_call(
        kernel,
        out_shape=jax.ShapeDtypeStruct((groups, outc, tok), jnp.float32),
        in_specs=[smem] * 3 + [anywhere] * 4 + [vmem] * 3,
        out_specs=vmem,
        scratch_shapes=[
            pltpu.VMEM((2, groups, rows, HD), jnp.bfloat16),
            pltpu.VMEM((groups, q_rows, HD), jnp.bfloat16),
            pltpu.VMEM((groups * tok, heads * HD), jnp.bfloat16),
            pltpu.SemaphoreType.DMA((3,)),
        ],
        compiler_params=pltpu.CompilerParams(vmem_limit_bytes=LIMIT),
        cost_estimate=pl.CostEstimate(flops=flops, bytes_accessed=4 * rows * groups * HD * 2, transcendentals=0),
    )(side, half, weight, own, before, after, queries, main_head, guide_heads, earlier)


def body(main_qkv, guide_qkv, main_head, guide_head, window_start, timestep):
    seq_index = lax.axis_index("seq")
    grp_index = lax.axis_index("grp")
    groups = lax.axis_size("grp")
    tok = main_qkv.shape[0]
    heads = main_head.shape[0] // HD
    assert groups * tok == TILE and window_start.shape[0] == lax.axis_size("seq")
    main = main_qkv.transpose(1, 0, 2)
    guide = guide_qkv.transpose(1, 0, 2)
    main_head = main_head.T
    guide_head = guide_head.T

    plan1, plan2, plan3 = [], [], []
    for g in range(groups):
        for h in range(heads):
            plan, at = (plan1, h) if h < FIRST else (plan2, h - FIRST)
            for kv in (0, 1):
                plan.append((0, 1 + kv, 0, tok, g * heads + h, g, (2 * at + kv) * tok))
            plan3.append((0, 0, 0, tok, g * heads + h, g, h * tok))
        whole, shared = guide_pair(g)
        base = 2 * (heads - FIRST)
        for i, (kv, head) in enumerate(((1, whole), (2, whole), (1, shared), (2, shared))):
            plan2.append((1, kv, 0, tok, head, g, (base + i) * tok))
        plan3.append((1, 0, 0, tok, whole, g, heads * tok))
        plan3.append((1, 0, (g % 2) * (tok // 2), tok // 2, shared, g, (heads + 1) * tok))
    own1 = swapped(pack([main], groups, plan1, 2 * FIRST * tok))
    own2 = swapped(pack([main, guide], groups, plan2, (2 * (heads - FIRST) + 4) * tok))
    queries = swapped(pack([main, guide], groups, plan3, (heads + 1) * tok + tok // 2))
    before1, after1 = passed_along(own1, "seq", 1), passed_along(own1, "seq", -1)
    before2, after2 = passed_along(own2, "seq", 1), passed_along(own2, "seq", -1)

    window_pos = lax.dynamic_slice_in_dim(window_start, seq_index, 1, 0)
    side = (window_pos == seq_index).astype(jnp.int32)
    half = (grp_index % 2).astype(jnp.int32).reshape(1)
    weight = 1.0 + 2.0 * timestep.astype(jnp.float32) / 999.0
    table = jnp.array([guide_pair(g) for g in range(groups)], jnp.int32)
    mine = lax.dynamic_index_in_dim(table, grp_index, 0, keepdims=False)
    guide_heads = jnp.concatenate(
        [lax.dynamic_slice_in_dim(guide_head, mine[i] * HD, HD, 1) for i in (0, 1)], axis=1
    )
    common = (main_head, guide_heads)
    nothing = jnp.zeros((1, 8, 128), jnp.float32)
    part = attention(side, half, weight, own1, before1, after1, queries, *common, nothing,
                     heads=FIRST, first_head=0, has_guide=False, tok=tok)
    part = attention(side, half, weight, own2, before2, after2, queries, *common, part,
                     heads=heads - FIRST, first_head=FIRST, has_guide=True, tok=tok)
    return jnp.sum(swapped(part), axis=0).T


def solution(mesh):
    in_specs = (
        P(("seq", "grp"), None, None),
        P(("seq", "grp"), None, None),
        P("grp", None),
        P(),
        P(),
        P(),
    )
    out_specs = P(("seq", "grp"), None)
    return jax.shard_map(body, mesh=mesh, in_specs=in_specs, out_specs=out_specs, check_vma=False)
```

```python
import math

import jax
import jax.numpy as jnp
from jax import lax
from jax.experimental import pallas as pl
from jax.experimental.pallas import tpu as pltpu
from jax.sharding import PartitionSpec as P

HD = 128
TILE = 384
SCALE = math.log2(math.e) / math.sqrt(HD)
LIMIT = 24 * 1024 * 1024
WIDE = 56 * 1024 * 1024
ANY = pl.BlockSpec(memory_space=pl.ANY)
HBM = pl.BlockSpec(memory_space=pltpu.HBM)
VMEM = pl.BlockSpec(memory_space=pltpu.VMEM)
SMEM = pl.BlockSpec(memory_space=pltpu.SMEM)


def traded(block, axis, first):
    lows = range(first, lax.axis_size(axis) - 1, 2)
    return lax.ppermute(block, axis, [p for i in lows for p in ((i, i + 1), (i + 1, i))])


def swapped(block):
    return lax.all_to_all(block, "grp", 0, 0)


def guide_pair(dst):
    return ((0, 1), (2, 1), (3, 4), (5, 4))[dst]


def times(left, right, dims):
    return lax.dot_general(left, right, (dims, ((), ())), preferred_element_type=jnp.float32)


def projected(values, head):
    return times(values, head, ((1,), (1,))).astype(jnp.bfloat16)


def pack(main, guide, guide_head, groups, heads):
    tok = main.shape[1]
    rows = (2 * heads + 3) * tok
    q_rows = (heads + 1) * tok + tok // 2
    half = guide_head.shape[0]

    def kernel(main_ref, guide_ref, heads_ref, out_ref, q_ref, m_buf, g_buf, head_ref, sem):
        order = (1, 2, 0)
        copies = [pltpu.make_async_copy(main_ref.at[i], m_buf.at[i], sem.at[i]) for i in order]
        copies += [pltpu.make_async_copy(guide_ref.at[i], g_buf.at[i], sem.at[3 + i]) for i in order]
        copies.append(pltpu.make_async_copy(heads_ref, head_ref, sem.at[6]))
        for copy in copies:
            copy.start()
        for i, copy in zip(order, copies):
            copy.wait()
            to = (q_ref, out_ref, out_ref)[i]
            for g in range(groups):
                for h in range(heads):
                    at = (h + (heads if i == 2 else 0)) * tok
                    to[g, pl.ds(at, tok), :] = m_buf[i, :, pl.ds((g * heads + h) * HD, HD)]
        for copy in copies[3:]:
            copy.wait()
        for g in range(groups):
            whole, shared = guide_pair(g)
            for i, head in enumerate((whole, shared)):
                cols = pl.ds(head * HD, HD)
                out_ref[g, pl.ds((2 * heads + i) * tok, tok), :] = g_buf[1, :, cols]
                out_ref[g, pl.ds((2 * heads + 2) * tok, tok), pl.ds(i * half, half)] = projected(
                    g_buf[2, :, cols], head_ref[:, cols]
                )
            q_ref[g, pl.ds(heads * tok, tok), :] = g_buf[0, :, pl.ds(whole * HD, HD)]
            q_ref[g, pl.ds((heads + 1) * tok, tok // 2), :] = g_buf[
                0, pl.ds((g % 2) * (tok // 2), tok // 2), pl.ds(shared * HD, HD)
            ]

    return pl.pallas_call(
        kernel,
        out_shape=[
            jax.ShapeDtypeStruct((groups, rows, HD), jnp.bfloat16),
            jax.ShapeDtypeStruct((groups, q_rows, HD), jnp.bfloat16),
        ],
        in_specs=[HBM, HBM, HBM],
        out_specs=[VMEM, VMEM],
        scratch_shapes=[
            pltpu.VMEM(main.shape, jnp.bfloat16),
            pltpu.VMEM(guide.shape, jnp.bfloat16),
            pltpu.VMEM(guide_head.shape, jnp.bfloat16),
            pltpu.SemaphoreType.DMA((7,)),
        ],
        compiler_params=pltpu.CompilerParams(vmem_limit_bytes=WIDE),
    )(main, guide, guide_head)


def project_values(own, main_head, heads, tok):
    groups = own.shape[0]
    half = main_head.shape[0]
    rows = heads * tok + heads * tok // 2 + 3 * tok

    def kernel(own_ref, heads_ref, out_ref, buf, head_ref, sem):
        copies = [
            pltpu.make_async_copy(own_ref, buf, sem.at[0]),
            pltpu.make_async_copy(heads_ref, head_ref, sem.at[1]),
        ]
        for copy in copies:
            copy.start()
        for copy in copies:
            copy.wait()
        out_ref[:, pl.ds(0, heads * tok), :] = buf[:, pl.ds(0, heads * tok), :]
        for h in range(heads):
            values = buf[:, pl.ds((heads + h) * tok, tok), :].reshape(groups * tok, HD)
            moved = projected(values, head_ref[:, pl.ds(h * HD, HD)]).reshape(groups, tok, half)
            at = (heads + h // 2) * tok
            if h == heads - 1 and h % 2 == 0:
                out_ref[:, pl.ds(at, tok // 2), pl.ds(0, half)] = moved[:, : tok // 2]
                out_ref[:, pl.ds(at, tok // 2), pl.ds(half, half)] = moved[:, tok // 2 :]
            else:
                out_ref[:, pl.ds(at, tok), pl.ds((h % 2) * half, half)] = moved
        out_ref[:, pl.ds(rows - 3 * tok, 3 * tok), :] = buf[:, pl.ds(2 * heads * tok, 3 * tok), :]

    return pl.pallas_call(
        kernel,
        out_shape=jax.ShapeDtypeStruct((groups, rows, HD), jnp.bfloat16),
        in_specs=[ANY, HBM],
        out_specs=VMEM,
        scratch_shapes=[
            pltpu.VMEM(own.shape, jnp.bfloat16),
            pltpu.VMEM(main_head.shape, jnp.bfloat16),
            pltpu.SemaphoreType.DMA((2,)),
        ],
        compiler_params=pltpu.CompilerParams(vmem_limit_bytes=LIMIT),
    )(own, main_head)


def attention(window_start, timestep, own, across, beside, queries, heads, tok, half):
    groups, rows, _ = own.shape
    q_rows = queries.shape[1]
    span = groups * tok
    units = [(h * tok, (heads + h // 2) * tok, h % 2, h * tok, tok) for h in range(heads)]
    units += [(rows - (3 - i) * tok, rows - tok, i, (heads + i) * tok, tok // (i + 1)) for i in (0, 1)]

    def kernel(start_ref, step_ref, own_ref, across_ref, beside_ref, q_ref, out_ref,
               kv, s_buf, w_buf, sem):
        tile = lax.axis_index("seq")
        beside = (start_ref[tile] == tile) == (lax.rem(tile, 2) == 0)
        pieces = [(0, heads * tok), (heads * tok, rows - heads * tok)]

        @pl.when(beside)
        def _():
            for i, (at, count) in enumerate(pieces):
                part = pl.ds(at, count)
                pltpu.make_async_copy(beside_ref.at[:, part], kv.at[:, part], sem.at[i]).start()

        @pl.when(jnp.logical_not(beside))
        def _():
            for i, (at, count) in enumerate(pieces):
                part = pl.ds(at, count)
                pltpu.make_async_copy(across_ref.at[:, part], kv.at[:, part], sem.at[i]).start()

        pltpu.make_async_copy(
            across_ref.at[:, pl.ds(*pieces[0])], kv.at[:, pl.ds(*pieces[0])], sem.at[0]
        ).wait()

        def keys(buf, u):
            return buf[:, pl.ds(units[u][0], tok), :].reshape(span, HD)

        def values(buf, u):
            _, at, side, *_ = units[u]
            if u == heads - 1 and u % 2 == 0:
                found = buf[:, pl.ds(at, tok // 2), :]
                found = jnp.concatenate([found[..., :half], found[..., half:]], axis=1)
            else:
                found = buf[:, pl.ds(at, tok), pl.ds(side * half, half)]
            return found.reshape(span, half)

        def score(u):
            _, _, _, at, count = units[u]
            query = q_ref[:, pl.ds(at, count), :].reshape(groups * count, HD)
            for i, buf in enumerate((own_ref, kv)):
                s_buf[u % 2, pl.ds(0, groups * count), pl.ds(i * span, span)] = times(
                    query, keys(buf, u), ((1,), (1,))
                )

        def soften(u):
            for at in range(0, groups * units[u][-1], 96):
                part = pl.ds(at, 96)
                scores = s_buf[u % 2, part, :]
                top = jnp.max(scores, axis=-1, keepdims=True)
                lifted = jnp.exp2((scores - top) * SCALE)
                share = 1.0 / jnp.sum(lifted, axis=-1, keepdims=True)
                w_buf[u % 2, part, :] = (lifted * share).astype(jnp.bfloat16)

        def mix(u):
            part = pl.ds(0, groups * units[u][-1])
            return sum(
                times(w_buf[u % 2, part, pl.ds(i * span, span)], values(buf, u), ((1,), (0,)))
                for i, buf in enumerate((own_ref, kv))
            )

        mixes = []
        score(0)
        for u in range(len(units)):
            if u + 1 < len(units):
                score(u + 1)
            soften(u)
            if u == 0:
                pltpu.make_async_copy(
                    across_ref.at[:, pl.ds(*pieces[1])], kv.at[:, pl.ds(*pieces[1])], sem.at[1]
                ).wait()
            mixes.append(mix(u))
        main = sum(mixes[1:heads], mixes[0])
        whole, shared = mixes[heads:]
        shared = shared.reshape(groups, tok // 2, half)
        blank = jnp.zeros_like(shared)
        upper = lax.rem(lax.axis_index("grp"), 2) != 0
        shared = jnp.concatenate(
            [jnp.where(upper, blank, shared), jnp.where(upper, shared, blank)], axis=1
        )
        w = 1.0 + 2.0 * step_ref[0].astype(jnp.float32) / 999.0
        for j in range(groups):
            part = slice(j * tok, (j + 1) * tok)
            out_ref[j] = (w * main[part] + (1.0 - w) * (whole[part] + shared[j])).T

    flops = int(4 * (heads + 1.5) * groups * tok * 2 * groups * tok * HD)
    return pl.pallas_call(
        kernel,
        out_shape=jax.ShapeDtypeStruct((groups, half, tok), jnp.float32),
        in_specs=[SMEM] * 2 + [VMEM, ANY, ANY, VMEM],
        out_specs=VMEM,
        scratch_shapes=[
            pltpu.VMEM((groups, rows, HD), jnp.bfloat16),
            pltpu.VMEM((2, span, 2 * span), jnp.float32),
            pltpu.VMEM((2, span, 2 * span), jnp.bfloat16),
            pltpu.SemaphoreType.DMA((4,)),
        ],
        compiler_params=pltpu.CompilerParams(vmem_limit_bytes=LIMIT),
        cost_estimate=pl.CostEstimate(flops=flops, bytes_accessed=3 * rows * groups * HD * 2, transcendentals=0),
    )(window_start, timestep, own, across, beside, queries)


def body(main_qkv, guide_qkv, main_head, guide_head, window_start, timestep):
    groups = lax.axis_size("grp")
    tok = main_qkv.shape[0]
    heads = main_head.shape[0] // HD
    half = main_head.shape[1]
    assert groups * tok == TILE and window_start.shape[0] == lax.axis_size("seq")
    main = main_qkv.transpose(1, 0, 2)
    guide = guide_qkv.transpose(1, 0, 2)

    keys, queries = pack(main, guide, guide_head.T, groups, heads)
    gathered = swapped(keys)
    own = project_values(gathered, main_head.T, heads, tok)
    across, beside = traded(own, "seq", 1), traded(own, "seq", 0)
    queries = swapped(queries)
    part = attention(window_start, timestep, own, across, beside, queries, heads, tok, half)
    return jnp.sum(swapped(part), axis=0).T


def solution(mesh):
    in_specs = (
        P(("seq", "grp"), None, None),
        P(("seq", "grp"), None, None),
        P("grp", None),
        P(),
        P(),
        P(),
    )
    out_specs = P(("seq", "grp"), None)
    return jax.shard_map(body, mesh=mesh, in_specs=in_specs, out_specs=out_specs, check_vma=False)
```

```python
import math

import jax
import jax.numpy as jnp
from jax import lax
from jax.experimental import pallas as pl
from jax.experimental.pallas import tpu as pltpu
from jax.sharding import PartitionSpec as P

HD = 128
TILE = 384
SCALE = math.log2(math.e) / math.sqrt(HD)
LIMIT = 16 * 1024 * 1024
WIDE = 56 * 1024 * 1024
ANY = pl.BlockSpec(memory_space=pl.ANY)
HBM = pl.BlockSpec(memory_space=pltpu.HBM)
VMEM = pl.BlockSpec(memory_space=pltpu.VMEM)
SMEM = pl.BlockSpec(memory_space=pltpu.SMEM)


def traded(block, axis, first):
    lows = range(first, lax.axis_size(axis) - 1, 2)
    return lax.ppermute(block, axis, [p for i in lows for p in ((i, i + 1), (i + 1, i))])


def swapped(block):
    return lax.all_to_all(block, "grp", 0, 0)


def guide_pair(dst):
    return ((0, 1), (2, 1), (3, 4), (5, 4))[dst]


def times(left, right, dims):
    return lax.dot_general(left, right, (dims, ((), ())), preferred_element_type=jnp.float32)


def projected(values, head):
    return times(values, head, ((1,), (1,))).astype(jnp.bfloat16)


def spread(source, target, first, groups, heads):
    tok = source.shape[0]
    for g in range(groups):
        for h in range(heads):
            target[g, pl.ds(first + h * tok, tok), :] = source[:, pl.ds((g * heads + h) * HD, HD)]


def pack_keys(main, guide, guide_head, groups, heads):
    tok = main.shape[1]
    rows = (2 * heads + 3) * tok
    half = guide_head.shape[0]

    def kernel(main_ref, guide_ref, heads_ref, out_ref, m_buf, g_buf, head_ref, buf, sem, out_sem):
        main_in = [pltpu.make_async_copy(main_ref.at[1 + i], m_buf.at[i], sem.at[i]) for i in (0, 1)]
        guide_in = [
            pltpu.make_async_copy(heads_ref, head_ref, sem.at[2]),
            pltpu.make_async_copy(guide_ref.at[pl.ds(1, 2)], g_buf, sem.at[3]),
        ]
        for copy in guide_in + main_in:
            copy.start()
        copies = []

        def put(first, count):
            part = pl.ds(first, count)
            copies.append(
                pltpu.make_async_copy(buf.at[:, part], out_ref.at[:, part], out_sem.at[len(copies)])
            )
            copies[-1].start()

        def guides():
            for copy in guide_in:
                copy.wait()
            for g in range(groups):
                for i, head in enumerate(guide_pair(g)):
                    cols = pl.ds(head * HD, HD)
                    buf[g, pl.ds((2 * heads + i) * tok, tok), :] = g_buf[0, :, cols]
                    buf[g, pl.ds((2 * heads + 2) * tok, tok), pl.ds(i * half, half)] = projected(
                        g_buf[1, :, cols], head_ref[:, cols]
                    )
            put(2 * heads * tok, 3 * tok)

        guides()
        for i, copy in enumerate(main_in):
            copy.wait()
            spread(m_buf.at[i], buf, i * heads * tok, groups, heads)
            put(i * heads * tok, heads * tok)
        for copy in copies:
            copy.wait()

    return pl.pallas_call(
        kernel,
        out_shape=jax.ShapeDtypeStruct((groups, rows, HD), jnp.bfloat16),
        in_specs=[HBM, HBM, HBM],
        out_specs=HBM,
        scratch_shapes=[
            pltpu.VMEM((2,) + main.shape[1:], jnp.bfloat16),
            pltpu.VMEM((2,) + guide.shape[1:], jnp.bfloat16),
            pltpu.VMEM(guide_head.shape, jnp.bfloat16),
            pltpu.VMEM((groups, rows, HD), jnp.bfloat16),
            pltpu.SemaphoreType.DMA((4,)),
            pltpu.SemaphoreType.DMA((3,)),
        ],
        compiler_params=pltpu.CompilerParams(vmem_limit_bytes=WIDE),
    )(main, guide, guide_head)


def pack_queries(main, guide, groups, heads):
    tok = main.shape[1]
    rows = (heads + 1) * tok + tok // 2

    def kernel(main_ref, guide_ref, out_ref, m_buf, g_buf, sem):
        copies = [
            pltpu.make_async_copy(main_ref.at[0], m_buf, sem.at[0]),
            pltpu.make_async_copy(guide_ref.at[0], g_buf, sem.at[1]),
        ]
        for copy in copies:
            copy.start()
        copies[0].wait()
        spread(m_buf, out_ref, 0, groups, heads)
        copies[1].wait()
        for g in range(groups):
            whole, shared = guide_pair(g)
            out_ref[g, pl.ds(heads * tok, tok), :] = g_buf[:, pl.ds(whole * HD, HD)]
            out_ref[g, pl.ds((heads + 1) * tok, tok // 2), :] = g_buf[
                pl.ds((g % 2) * (tok // 2), tok // 2), pl.ds(shared * HD, HD)
            ]

    return pl.pallas_call(
        kernel,
        out_shape=jax.ShapeDtypeStruct((groups, rows, HD), jnp.bfloat16),
        in_specs=[HBM, HBM],
        out_specs=VMEM,
        scratch_shapes=[
            pltpu.VMEM(main.shape[1:], jnp.bfloat16),
            pltpu.VMEM(guide.shape[1:], jnp.bfloat16),
            pltpu.SemaphoreType.DMA((2,)),
        ],
        compiler_params=pltpu.CompilerParams(vmem_limit_bytes=WIDE),
    )(main, guide)


def project_values(own, main_head, heads, tok, after):
    groups = own.shape[0]
    half = main_head.shape[0]
    rows = heads * tok + heads * tok // 2 + 3 * tok

    def kernel(own_ref, head_ref, after_ref, out_ref):
        out_ref[:, pl.ds(0, heads * tok), :] = own_ref[:, pl.ds(0, heads * tok), :]
        for h in range(heads):
            values = own_ref[:, pl.ds((heads + h) * tok, tok), :].reshape(groups * tok, HD)
            moved = projected(values, head_ref[:, pl.ds(h * HD, HD)]).reshape(groups, tok, half)
            at = (heads + h // 2) * tok
            if h == heads - 1 and h % 2 == 0:
                out_ref[:, pl.ds(at, tok // 2), pl.ds(0, half)] = moved[:, : tok // 2]
                out_ref[:, pl.ds(at, tok // 2), pl.ds(half, half)] = moved[:, tok // 2 :]
            else:
                out_ref[:, pl.ds(at, tok), pl.ds((h % 2) * half, half)] = moved
        out_ref[:, pl.ds(rows - 3 * tok, 3 * tok), :] = own_ref[:, pl.ds(2 * heads * tok, 3 * tok), :]

    return pl.pallas_call(
        kernel,
        out_shape=jax.ShapeDtypeStruct((groups, rows, HD), jnp.bfloat16),
        in_specs=[VMEM, VMEM, ANY],
        out_specs=VMEM,
        compiler_params=pltpu.CompilerParams(vmem_limit_bytes=LIMIT),
    )(own, main_head, after)


def cut(block, bounds):
    groups = block.shape[0]
    counts = [b - a for a, b in zip(bounds, bounds[1:])]

    def kernel(ref, *refs):
        outs, sem = refs[:-1], refs[-1]
        copies = [
            pltpu.make_async_copy(ref.at[:, pl.ds(a, count)], out, sem.at[i])
            for i, (a, count, out) in enumerate(zip(bounds, counts, outs))
        ]
        for copy in copies:
            copy.start()
        for copy in copies:
            copy.wait()

    return pl.pallas_call(
        kernel,
        out_shape=[jax.ShapeDtypeStruct((groups, count, HD), jnp.bfloat16) for count in counts],
        in_specs=[ANY],
        out_specs=[ANY] * len(counts),
        scratch_shapes=[pltpu.SemaphoreType.DMA((len(counts),))],
        compiler_params=pltpu.CompilerParams(vmem_limit_bytes=LIMIT),
    )(block)


def attention(window_start, timestep, own, across, beside, queries, heads, tok, half):
    groups, rows, _ = own.shape
    span = groups * tok
    units = [(h * tok, (heads + h // 2) * tok, h % 2, h * tok, tok) for h in range(heads)]
    units += [(rows - (3 - i) * tok, rows - tok, i, (heads + i) * tok, tok // (i + 1)) for i in (0, 1)]

    def kernel(start_ref, step_ref, own_ref, across_ref, *refs):
        beside_refs, (q_ref, out_ref, s_buf, w_buf) = refs[: len(beside)], refs[len(beside) :]
        tile = lax.axis_index("seq")

        def block(parts, at, count):
            for part in parts:
                if at < part.shape[1]:
                    return part[:, pl.ds(at, count), :]
                at -= part.shape[1]

        def keys(parts, u):
            return block(parts, units[u][0], tok).reshape(span, HD)

        def values(parts, u):
            _, at, side, *_ = units[u]
            if u == heads - 1 and u % 2 == 0:
                found = block(parts, at, tok // 2)
                found = jnp.concatenate([found[..., :half], found[..., half:]], axis=1)
            else:
                found = block(parts, at, tok)[..., side * half : (side + 1) * half]
            return found.reshape(span, half)

        def attend(sources):
            def score(u):
                _, _, _, at, count = units[u]
                query = q_ref[:, pl.ds(at, count), :].reshape(groups * count, HD)
                for i, parts in enumerate(sources):
                    s_buf[u % 2, pl.ds(0, groups * count), pl.ds(i * span, span)] = times(
                        query, keys(parts, u), ((1,), (1,))
                    )

            def soften(u):
                for at in range(0, groups * units[u][-1], tok):
                    part = pl.ds(at, tok)
                    scores = s_buf[u % 2, part, :]
                    top = jnp.max(scores, axis=-1, keepdims=True)
                    lifted = jnp.exp2((scores - top) * SCALE)
                    share = 1.0 / jnp.sum(lifted, axis=-1, keepdims=True)
                    w_buf[u % 2, part, :] = (lifted * share).astype(jnp.bfloat16)

            def mix(u):
                part = pl.ds(0, groups * units[u][-1])
                both = jnp.concatenate([values(parts, u) for parts in sources], axis=0)
                return times(w_buf[u % 2, part, :], both, ((1,), (0,)))

            mixes = []
            score(0)
            for u in range(len(units)):
                if u + 1 < len(units):
                    score(u + 1)
                soften(u)
                mixes.append(mix(u))
            main = sum(mixes[1:heads], mixes[0])
            whole, shared = mixes[heads:]
            shared = shared.reshape(groups, tok // 2, half)
            blank = jnp.zeros_like(shared)
            upper = lax.rem(lax.axis_index("grp"), 2) != 0
            shared = jnp.concatenate(
                [jnp.where(upper, blank, shared), jnp.where(upper, shared, blank)], axis=1
            )
            w = 1.0 + 2.0 * step_ref[0].astype(jnp.float32) / 999.0
            for j in range(groups):
                part = slice(j * tok, (j + 1) * tok)
                out_ref[j] = (w * main[part] + (1.0 - w) * (whole[part] + shared[j])).T

        use_beside = (start_ref[tile] == tile) == (lax.rem(tile, 2) == 0)

        @pl.when(use_beside)
        def _():
            attend(([own_ref], beside_refs))

        @pl.when(jnp.logical_not(use_beside))
        def _():
            attend(([own_ref], [across_ref]))

    flops = int(4 * (heads + 1.5) * groups * tok * 2 * groups * tok * HD)
    return pl.pallas_call(
        kernel,
        out_shape=jax.ShapeDtypeStruct((groups, half, tok), jnp.float32),
        in_specs=[SMEM] * 2 + [VMEM] * (3 + len(beside)),
        out_specs=VMEM,
        scratch_shapes=[
            pltpu.VMEM((2, span, 2 * span), jnp.float32),
            pltpu.VMEM((2, span, 2 * span), jnp.bfloat16),
        ],
        compiler_params=pltpu.CompilerParams(vmem_limit_bytes=LIMIT),
        cost_estimate=pl.CostEstimate(flops=flops, bytes_accessed=3 * rows * groups * HD * 2, transcendentals=0),
    )(window_start, timestep, own, across, *beside, queries)


def body(main_qkv, guide_qkv, main_head, guide_head, window_start, timestep):
    groups = lax.axis_size("grp")
    tok = main_qkv.shape[0]
    heads = main_head.shape[0] // HD
    half = main_head.shape[1]
    assert groups * tok == TILE and window_start.shape[0] == lax.axis_size("seq")
    main = main_qkv.transpose(1, 0, 2)
    guide = guide_qkv.transpose(1, 0, 2)

    packed = pack_queries(main, guide, groups, heads)
    gathered = swapped(pack_keys(main, guide, guide_head.T, groups, heads))
    own = project_values(gathered, main_head.T, heads, tok, packed)
    across = traded(own, "seq", 1)
    beside = [traded(part, "seq", 0) for part in cut(own, (0, 3 * tok, 6 * tok, own.shape[1]))]
    queries = swapped(packed)
    part = attention(window_start, timestep, own, across, beside, queries, heads, tok, half)
    return jnp.sum(swapped(part), axis=0).T


def solution(mesh):
    in_specs = (
        P(("seq", "grp"), None, None),
        P(("seq", "grp"), None, None),
        P("grp", None),
        P(),
        P(),
        P(),
    )
    out_specs = P(("seq", "grp"), None)
    return jax.shard_map(body, mesh=mesh, in_specs=in_specs, out_specs=out_specs, check_vma=False)
```

```python
import math

import jax
import jax.numpy as jnp
from jax import lax
from jax.experimental import pallas as pl
from jax.experimental.pallas import tpu as pltpu
from jax.sharding import PartitionSpec as P

HD = 128
TILE = 384
SCALE = math.log2(math.e) / math.sqrt(HD)
LIMIT = 16 * 1024 * 1024
WIDE = 56 * 1024 * 1024
ANY = pl.BlockSpec(memory_space=pl.ANY)
HBM = pl.BlockSpec(memory_space=pltpu.HBM)
VMEM = pl.BlockSpec(memory_space=pltpu.VMEM)
SMEM = pl.BlockSpec(memory_space=pltpu.SMEM)


def traded(block, axis, first):
    lows = range(first, lax.axis_size(axis) - 1, 2)
    return lax.ppermute(block, axis, [p for i in lows for p in ((i, i + 1), (i + 1, i))])


def swapped(block):
    return lax.all_to_all(block, "grp", 0, 0)


def guide_pair(dst):
    return ((0, 1), (2, 1), (3, 4), (5, 4))[dst]


def times(left, right, dims):
    return lax.dot_general(left, right, (dims, ((), ())), preferred_element_type=jnp.float32)


def projected(values, head):
    return times(values, head, ((1,), (1,))).astype(jnp.bfloat16)


def spread(source, target, first, groups, heads):
    tok = source.shape[0]
    for g in range(groups):
        for h in range(heads):
            target[g, pl.ds(first + h * tok, tok), :] = source[:, pl.ds((g * heads + h) * HD, HD)]


def pack_keys(main, guide, guide_head, groups, heads):
    tok = main.shape[1]
    rows = (2 * heads + 3) * tok
    half = guide_head.shape[0]

    def kernel(main_ref, guide_ref, heads_ref, out_ref, m_buf, g_buf, head_ref, buf, sem, out_sem):
        main_in = [pltpu.make_async_copy(main_ref.at[1 + i], m_buf.at[i], sem.at[i]) for i in (0, 1)]
        guide_in = [
            pltpu.make_async_copy(heads_ref, head_ref, sem.at[2]),
            pltpu.make_async_copy(guide_ref.at[pl.ds(1, 2)], g_buf, sem.at[3]),
        ]
        for copy in guide_in + main_in:
            copy.start()
        copies = []

        def put(first, count):
            part = pl.ds(first, count)
            copies.append(
                pltpu.make_async_copy(buf.at[:, part], out_ref.at[:, part], out_sem.at[len(copies)])
            )
            copies[-1].start()

        def guides():
            for copy in guide_in:
                copy.wait()
            for g in range(groups):
                for i, head in enumerate(guide_pair(g)):
                    cols = pl.ds(head * HD, HD)
                    buf[g, pl.ds((2 * heads + i) * tok, tok), :] = g_buf[0, :, cols]
                    buf[g, pl.ds((2 * heads + 2) * tok, tok), pl.ds(i * half, half)] = projected(
                        g_buf[1, :, cols], head_ref[:, cols]
                    )
            put(2 * heads * tok, 3 * tok)

        guides()
        for i, copy in enumerate(main_in):
            copy.wait()
            spread(m_buf.at[i], buf, i * heads * tok, groups, heads)
            put(i * heads * tok, heads * tok)
        for copy in copies:
            copy.wait()

    return pl.pallas_call(
        kernel,
        out_shape=jax.ShapeDtypeStruct((groups, rows, HD), jnp.bfloat16),
        in_specs=[HBM, HBM, HBM],
        out_specs=HBM,
        scratch_shapes=[
            pltpu.VMEM((2,) + main.shape[1:], jnp.bfloat16),
            pltpu.VMEM((2,) + guide.shape[1:], jnp.bfloat16),
            pltpu.VMEM(guide_head.shape, jnp.bfloat16),
            pltpu.VMEM((groups, rows, HD), jnp.bfloat16),
            pltpu.SemaphoreType.DMA((4,)),
            pltpu.SemaphoreType.DMA((3,)),
        ],
        compiler_params=pltpu.CompilerParams(vmem_limit_bytes=WIDE),
    )(main, guide, guide_head)


def pack_queries(main, guide, groups, heads):
    tok = main.shape[1]
    rows = (heads + 1) * tok + tok // 2

    def kernel(main_ref, guide_ref, out_ref, m_buf, g_buf, sem):
        copies = [
            pltpu.make_async_copy(main_ref.at[0], m_buf, sem.at[0]),
            pltpu.make_async_copy(guide_ref.at[0], g_buf, sem.at[1]),
        ]
        for copy in copies:
            copy.start()
        copies[0].wait()
        spread(m_buf, out_ref, 0, groups, heads)
        copies[1].wait()
        for g in range(groups):
            whole, shared = guide_pair(g)
            out_ref[g, pl.ds(heads * tok, tok), :] = g_buf[:, pl.ds(whole * HD, HD)]
            out_ref[g, pl.ds((heads + 1) * tok, tok // 2), :] = g_buf[
                pl.ds((g % 2) * (tok // 2), tok // 2), pl.ds(shared * HD, HD)
            ]

    return pl.pallas_call(
        kernel,
        out_shape=jax.ShapeDtypeStruct((groups, rows, HD), jnp.bfloat16),
        in_specs=[HBM, HBM],
        out_specs=VMEM,
        scratch_shapes=[
            pltpu.VMEM(main.shape[1:], jnp.bfloat16),
            pltpu.VMEM(guide.shape[1:], jnp.bfloat16),
            pltpu.SemaphoreType.DMA((2,)),
        ],
        compiler_params=pltpu.CompilerParams(vmem_limit_bytes=WIDE),
    )(main, guide)


def project_values(own, main_head, heads, tok, after):
    groups = own.shape[0]
    half = main_head.shape[0]
    rows = heads * tok + heads * tok // 2 + 3 * tok

    def kernel(own_ref, head_ref, after_ref, out_ref):
        out_ref[:, pl.ds(0, heads * tok), :] = own_ref[:, pl.ds(0, heads * tok), :]
        for h in range(heads):
            values = own_ref[:, pl.ds((heads + h) * tok, tok), :].reshape(groups * tok, HD)
            moved = projected(values, head_ref[:, pl.ds(h * HD, HD)]).reshape(groups, tok, half)
            at = (heads + h // 2) * tok
            if h == heads - 1 and h % 2 == 0:
                out_ref[:, pl.ds(at, tok // 2), pl.ds(0, half)] = moved[:, : tok // 2]
                out_ref[:, pl.ds(at, tok // 2), pl.ds(half, half)] = moved[:, tok // 2 :]
            else:
                out_ref[:, pl.ds(at, tok), pl.ds((h % 2) * half, half)] = moved
        out_ref[:, pl.ds(rows - 3 * tok, 3 * tok), :] = own_ref[:, pl.ds(2 * heads * tok, 3 * tok), :]

    return pl.pallas_call(
        kernel,
        out_shape=jax.ShapeDtypeStruct((groups, rows, HD), jnp.bfloat16),
        in_specs=[VMEM, VMEM, ANY],
        out_specs=VMEM,
        compiler_params=pltpu.CompilerParams(vmem_limit_bytes=LIMIT),
    )(own, main_head, after)


def cut(block, bounds):
    groups = block.shape[0]
    counts = [b - a for a, b in zip(bounds, bounds[1:])]

    def kernel(ref, *refs):
        outs, sem = refs[:-1], refs[-1]
        copies = [
            pltpu.make_async_copy(ref.at[:, pl.ds(a, count)], out, sem.at[i])
            for i, (a, count, out) in enumerate(zip(bounds, counts, outs))
        ]
        for copy in copies:
            copy.start()
        for copy in copies:
            copy.wait()

    return pl.pallas_call(
        kernel,
        out_shape=[jax.ShapeDtypeStruct((groups, count, HD), jnp.bfloat16) for count in counts],
        in_specs=[ANY],
        out_specs=[ANY] * len(counts),
        scratch_shapes=[pltpu.SemaphoreType.DMA((len(counts),))],
        compiler_params=pltpu.CompilerParams(vmem_limit_bytes=LIMIT),
    )(block)


def attention(window_start, timestep, own, across, beside, queries, heads, tok, half):
    groups, rows, _ = own.shape
    span = groups * tok
    units = [(h * tok, (heads + h // 2) * tok, h % 2, h * tok, tok) for h in range(heads)]
    units += [(rows - (3 - i) * tok, rows - tok, i, (heads + i) * tok, tok // (i + 1)) for i in (0, 1)]

    def kernel(start_ref, step_ref, own_ref, across_ref, *refs):
        beside_refs, (q_ref, out_ref, s_buf, w_buf) = refs[: len(beside)], refs[len(beside) :]
        tile = lax.axis_index("seq")

        def block(parts, at, count):
            for part in parts:
                if at < part.shape[1]:
                    return part[:, pl.ds(at, count), :]
                at -= part.shape[1]

        def keys(parts, u):
            return block(parts, units[u][0], tok).reshape(span, HD)

        def values(parts, u):
            _, at, side, *_ = units[u]
            if u == heads - 1 and u % 2 == 0:
                found = block(parts, at, tok // 2)
                found = jnp.concatenate([found[..., :half], found[..., half:]], axis=1)
            else:
                found = block(parts, at, tok)[..., side * half : (side + 1) * half]
            return found.reshape(span, half)

        def attend(sources):
            def score(u):
                _, _, _, at, count = units[u]
                query = q_ref[:, pl.ds(at, count), :].reshape(groups * count, HD)
                for i, parts in enumerate(sources):
                    s_buf[u % 2, pl.ds(0, groups * count), pl.ds(i * span, span)] = times(
                        query, keys(parts, u), ((1,), (1,))
                    )

            def soften(u):
                for at in range(0, groups * units[u][-1], 2 * tok):
                    part = pl.ds(at, 2 * tok)
                    scores = s_buf[u % 2, part, :]
                    top = jnp.max(scores, axis=-1, keepdims=True)
                    lifted = jnp.exp2((scores - top) * SCALE)
                    share = 1.0 / jnp.sum(lifted, axis=-1, keepdims=True)
                    w_buf[u % 2, part, :] = (lifted * share).astype(jnp.bfloat16)

            def mix(u):
                part = pl.ds(0, groups * units[u][-1])
                both = jnp.concatenate([values(parts, u) for parts in sources], axis=0)
                return times(w_buf[u % 2, part, :], both, ((1,), (0,)))

            mixes = []
            score(0)
            for u in range(len(units)):
                if u + 1 < len(units):
                    score(u + 1)
                if u:
                    mixes.append(mix(u - 1))
                soften(u)
            mixes.append(mix(len(units) - 1))
            main = sum(mixes[1:heads], mixes[0])
            whole, shared = mixes[heads:]
            shared = shared.reshape(groups, tok // 2, half)
            blank = jnp.zeros_like(shared)
            upper = lax.rem(lax.axis_index("grp"), 2) != 0
            shared = jnp.concatenate(
                [jnp.where(upper, blank, shared), jnp.where(upper, shared, blank)], axis=1
            )
            w = 1.0 + 2.0 * step_ref[0].astype(jnp.float32) / 999.0
            for j in range(groups):
                part = slice(j * tok, (j + 1) * tok)
                out_ref[j] = (w * main[part] + (1.0 - w) * (whole[part] + shared[j])).T

        use_beside = (start_ref[tile] == tile) == (lax.rem(tile, 2) == 0)

        @pl.when(use_beside)
        def _():
            attend(([own_ref], beside_refs))

        @pl.when(jnp.logical_not(use_beside))
        def _():
            attend(([own_ref], [across_ref]))

    flops = int(4 * (heads + 1.5) * groups * tok * 2 * groups * tok * HD)
    return pl.pallas_call(
        kernel,
        out_shape=jax.ShapeDtypeStruct((groups, half, tok), jnp.float32),
        in_specs=[SMEM] * 2 + [VMEM] * (3 + len(beside)),
        out_specs=VMEM,
        scratch_shapes=[
            pltpu.VMEM((2, span, 2 * span), jnp.float32),
            pltpu.VMEM((2, span, 2 * span), jnp.bfloat16),
        ],
        compiler_params=pltpu.CompilerParams(vmem_limit_bytes=LIMIT),
        cost_estimate=pl.CostEstimate(flops=flops, bytes_accessed=3 * rows * groups * HD * 2, transcendentals=0),
    )(window_start, timestep, own, across, *beside, queries)


def body(main_qkv, guide_qkv, main_head, guide_head, window_start, timestep):
    groups = lax.axis_size("grp")
    tok = main_qkv.shape[0]
    heads = main_head.shape[0] // HD
    half = main_head.shape[1]
    assert groups * tok == TILE and window_start.shape[0] == lax.axis_size("seq")
    main = main_qkv.transpose(1, 0, 2)
    guide = guide_qkv.transpose(1, 0, 2)

    packed = pack_queries(main, guide, groups, heads)
    gathered = swapped(pack_keys(main, guide, guide_head.T, groups, heads))
    own = project_values(gathered, main_head.T, heads, tok, packed)
    across = traded(own, "seq", 1)
    beside = [traded(part, "seq", 0) for part in cut(own, (0, 4 * tok, own.shape[1] - 2 * tok, own.shape[1]))]
    queries = swapped(packed)
    part = attention(window_start, timestep, own, across, beside, queries, heads, tok, half)
    return jnp.sum(swapped(part), axis=0).T


def solution(mesh):
    in_specs = (
        P(("seq", "grp"), None, None),
        P(("seq", "grp"), None, None),
        P("grp", None),
        P(),
        P(),
        P(),
    )
    out_specs = P(("seq", "grp"), None)
    return jax.shard_map(body, mesh=mesh, in_specs=in_specs, out_specs=out_specs, check_vma=False)
```

```python
import math

import jax
import jax.numpy as jnp
from jax import lax
from jax.experimental import pallas as pl
from jax.experimental.pallas import tpu as pltpu
from jax.sharding import PartitionSpec as P

HD = 128
TILE = 384
SCALE = math.log2(math.e) / math.sqrt(HD)
LIMIT = 16 * 1024 * 1024
WIDE = 56 * 1024 * 1024
ANY = pl.BlockSpec(memory_space=pl.ANY)
HBM = pl.BlockSpec(memory_space=pltpu.HBM)
VMEM = pl.BlockSpec(memory_space=pltpu.VMEM)
SMEM = pl.BlockSpec(memory_space=pltpu.SMEM)


def traded(block, axis, first):
    lows = range(first, lax.axis_size(axis) - 1, 2)
    return lax.ppermute(block, axis, [p for i in lows for p in ((i, i + 1), (i + 1, i))])


def swapped(block):
    return lax.all_to_all(block, "grp", 0, 0)


def guide_pair(dst):
    return ((0, 1), (2, 1), (3, 4), (5, 4))[dst]


def times(left, right, dims):
    return lax.dot_general(left, right, (dims, ((), ())), preferred_element_type=jnp.float32)


def projected(values, head):
    return times(values, head, ((1,), (1,))).astype(jnp.bfloat16)


def spread(source, target, first, groups, heads):
    tok = source.shape[0]
    for g in range(groups):
        for h in range(heads):
            target[g, pl.ds(first + h * tok, tok), :] = source[:, pl.ds((g * heads + h) * HD, HD)]


def pack_keys(main, guide, guide_head, groups, heads):
    tok = main.shape[1]
    rows = (2 * heads + 3) * tok
    half = guide_head.shape[0]

    def kernel(main_ref, guide_ref, heads_ref, out_ref, m_buf, g_buf, head_ref, buf, sem, out_sem):
        main_in = [pltpu.make_async_copy(main_ref.at[1 + i], m_buf.at[i], sem.at[i]) for i in (0, 1)]
        guide_in = [
            pltpu.make_async_copy(heads_ref, head_ref, sem.at[2]),
            pltpu.make_async_copy(guide_ref.at[pl.ds(1, 2)], g_buf, sem.at[3]),
        ]
        for copy in guide_in + main_in:
            copy.start()
        copies = []

        def put(first, count):
            part = pl.ds(first, count)
            copies.append(
                pltpu.make_async_copy(buf.at[:, part], out_ref.at[:, part], out_sem.at[len(copies)])
            )
            copies[-1].start()

        def guides():
            for copy in guide_in:
                copy.wait()
            for g in range(groups):
                for i, head in enumerate(guide_pair(g)):
                    cols = pl.ds(head * HD, HD)
                    buf[g, pl.ds((2 * heads + i) * tok, tok), :] = g_buf[0, :, cols]
                    buf[g, pl.ds((2 * heads + 2) * tok, tok), pl.ds(i * half, half)] = projected(
                        g_buf[1, :, cols], head_ref[:, cols]
                    )
            put(2 * heads * tok, 3 * tok)

        guides()
        for i, copy in enumerate(main_in):
            copy.wait()
            spread(m_buf.at[i], buf, i * heads * tok, groups, heads)
            put(i * heads * tok, heads * tok)
        for copy in copies:
            copy.wait()

    return pl.pallas_call(
        kernel,
        out_shape=jax.ShapeDtypeStruct((groups, rows, HD), jnp.bfloat16),
        in_specs=[HBM, HBM, HBM],
        out_specs=HBM,
        scratch_shapes=[
            pltpu.VMEM((2,) + main.shape[1:], jnp.bfloat16),
            pltpu.VMEM((2,) + guide.shape[1:], jnp.bfloat16),
            pltpu.VMEM(guide_head.shape, jnp.bfloat16),
            pltpu.VMEM((groups, rows, HD), jnp.bfloat16),
            pltpu.SemaphoreType.DMA((4,)),
            pltpu.SemaphoreType.DMA((3,)),
        ],
        compiler_params=pltpu.CompilerParams(vmem_limit_bytes=WIDE),
    )(main, guide, guide_head)


def pack_queries(main, guide, groups, heads):
    tok = main.shape[1]
    rows = (heads + 1) * tok + tok // 2

    def kernel(main_ref, guide_ref, out_ref, m_buf, g_buf, sem):
        copies = [
            pltpu.make_async_copy(main_ref.at[0], m_buf, sem.at[0]),
            pltpu.make_async_copy(guide_ref.at[0], g_buf, sem.at[1]),
        ]
        for copy in copies:
            copy.start()
        copies[0].wait()
        spread(m_buf, out_ref, 0, groups, heads)
        copies[1].wait()
        for g in range(groups):
            whole, shared = guide_pair(g)
            out_ref[g, pl.ds(heads * tok, tok), :] = g_buf[:, pl.ds(whole * HD, HD)]
            out_ref[g, pl.ds((heads + 1) * tok, tok // 2), :] = g_buf[
                pl.ds((g % 2) * (tok // 2), tok // 2), pl.ds(shared * HD, HD)
            ]

    return pl.pallas_call(
        kernel,
        out_shape=jax.ShapeDtypeStruct((groups, rows, HD), jnp.bfloat16),
        in_specs=[HBM, HBM],
        out_specs=VMEM,
        scratch_shapes=[
            pltpu.VMEM(main.shape[1:], jnp.bfloat16),
            pltpu.VMEM(guide.shape[1:], jnp.bfloat16),
            pltpu.SemaphoreType.DMA((2,)),
        ],
        compiler_params=pltpu.CompilerParams(vmem_limit_bytes=WIDE),
    )(main, guide)


def project_values(own, main_head, heads, tok, after):
    groups = own.shape[0]
    half = main_head.shape[0]
    rows = heads * tok + heads * tok // 2 + 3 * tok

    def kernel(own_ref, head_ref, after_ref, out_ref):
        out_ref[:, pl.ds(0, heads * tok), :] = own_ref[:, pl.ds(0, heads * tok), :]
        for h in range(heads):
            values = own_ref[:, pl.ds((heads + h) * tok, tok), :].reshape(groups * tok, HD)
            moved = projected(values, head_ref[:, pl.ds(h * HD, HD)]).reshape(groups, tok, half)
            at = (heads + h // 2) * tok
            if h == heads - 1 and h % 2 == 0:
                out_ref[:, pl.ds(at, tok // 2), pl.ds(0, half)] = moved[:, : tok // 2]
                out_ref[:, pl.ds(at, tok // 2), pl.ds(half, half)] = moved[:, tok // 2 :]
            else:
                out_ref[:, pl.ds(at, tok), pl.ds((h % 2) * half, half)] = moved
        out_ref[:, pl.ds(rows - 3 * tok, 3 * tok), :] = own_ref[:, pl.ds(2 * heads * tok, 3 * tok), :]

    return pl.pallas_call(
        kernel,
        out_shape=jax.ShapeDtypeStruct((groups, rows, HD), jnp.bfloat16),
        in_specs=[VMEM, VMEM, ANY],
        out_specs=VMEM,
        compiler_params=pltpu.CompilerParams(vmem_limit_bytes=LIMIT),
    )(own, main_head, after)


def cut(block, bounds):
    groups = block.shape[0]
    counts = [b - a for a, b in zip(bounds, bounds[1:])]

    def kernel(ref, *refs):
        outs, sem = refs[:-1], refs[-1]
        copies = [
            pltpu.make_async_copy(ref.at[:, pl.ds(a, count)], out, sem.at[i])
            for i, (a, count, out) in enumerate(zip(bounds, counts, outs))
        ]
        for copy in copies:
            copy.start()
        for copy in copies:
            copy.wait()

    return pl.pallas_call(
        kernel,
        out_shape=[jax.ShapeDtypeStruct((groups, count, HD), jnp.bfloat16) for count in counts],
        in_specs=[ANY],
        out_specs=[ANY] * len(counts),
        scratch_shapes=[pltpu.SemaphoreType.DMA((len(counts),))],
        compiler_params=pltpu.CompilerParams(vmem_limit_bytes=LIMIT),
    )(block)


def attention(window_start, timestep, own, across, beside, queries, heads, tok, half):
    groups, rows, _ = own.shape
    span = groups * tok
    units = [(h * tok, (heads + h // 2) * tok, h % 2, h * tok, tok) for h in range(heads)]
    units += [(rows - (3 - i) * tok, rows - tok, i, (heads + i) * tok, tok // (i + 1)) for i in (0, 1)]

    def kernel(start_ref, step_ref, own_ref, across_ref, *refs):
        beside_refs, (q_ref, out_ref, s_buf, w_buf) = refs[: len(beside)], refs[len(beside) :]
        tile = lax.axis_index("seq")

        def block(parts, at, count):
            for part in parts:
                if at < part.shape[1]:
                    return part[:, pl.ds(at, count), :]
                at -= part.shape[1]

        def keys(parts, u):
            return block(parts, units[u][0], tok).reshape(span, HD)

        def values(parts, u):
            _, at, side, *_ = units[u]
            if u == heads - 1 and u % 2 == 0:
                found = block(parts, at, tok // 2)
                found = jnp.concatenate([found[..., :half], found[..., half:]], axis=1)
            else:
                found = block(parts, at, tok)[..., side * half : (side + 1) * half]
            return found.reshape(span, half)

        def attend(sources):
            def score(u):
                _, _, _, at, count = units[u]
                query = q_ref[:, pl.ds(at, count), :].reshape(groups * count, HD)
                for i, parts in enumerate(sources):
                    s_buf[u % 2, pl.ds(0, groups * count), pl.ds(i * span, span)] = times(
                        query, keys(parts, u), ((1,), (1,))
                    )

            def soften(u):
                for at in range(0, groups * units[u][-1], 2 * tok):
                    part = pl.ds(at, 2 * tok)
                    scores = s_buf[u % 2, part, :]
                    top = jnp.max(scores, axis=-1, keepdims=True)
                    lifted = jnp.exp2((scores - top) * SCALE)
                    share = 1.0 / jnp.sum(lifted, axis=-1, keepdims=True)
                    w_buf[u % 2, part, :] = (lifted * share).astype(jnp.bfloat16)

            def mix(u):
                part = pl.ds(0, groups * units[u][-1])
                both = jnp.concatenate([values(parts, u) for parts in sources], axis=0)
                return times(w_buf[u % 2, part, :], both, ((1,), (0,)))

            mixes = []
            score(0)
            for u in range(len(units)):
                if u + 1 < len(units):
                    score(u + 1)
                if u:
                    mixes.append(mix(u - 1))
                soften(u)
            mixes.append(mix(len(units) - 1))
            main = sum(mixes[1:heads], mixes[0])
            whole, shared = mixes[heads:]
            shared = shared.reshape(groups, tok // 2, half)
            blank = jnp.zeros_like(shared)
            upper = lax.rem(lax.axis_index("grp"), 2) != 0
            shared = jnp.concatenate(
                [jnp.where(upper, blank, shared), jnp.where(upper, shared, blank)], axis=1
            )
            w = 1.0 + 2.0 * step_ref[0].astype(jnp.float32) / 999.0
            for j in range(groups):
                part = slice(j * tok, (j + 1) * tok)
                out_ref[j] = (w * main[part] + (1.0 - w) * (whole[part] + shared[j])).T.astype(jnp.bfloat16)

        use_beside = (start_ref[tile] == tile) == (lax.rem(tile, 2) == 0)

        @pl.when(use_beside)
        def _():
            attend(([own_ref], beside_refs))

        @pl.when(jnp.logical_not(use_beside))
        def _():
            attend(([own_ref], [across_ref]))

    flops = int(4 * (heads + 1.5) * groups * tok * 2 * groups * tok * HD)
    return pl.pallas_call(
        kernel,
        out_shape=jax.ShapeDtypeStruct((groups, half, tok), jnp.bfloat16),
        in_specs=[SMEM] * 2 + [VMEM] * (3 + len(beside)),
        out_specs=VMEM,
        scratch_shapes=[
            pltpu.VMEM((2, span, 2 * span), jnp.float32),
            pltpu.VMEM((2, span, 2 * span), jnp.bfloat16),
        ],
        compiler_params=pltpu.CompilerParams(vmem_limit_bytes=LIMIT),
        cost_estimate=pl.CostEstimate(flops=flops, bytes_accessed=3 * rows * groups * HD * 2, transcendentals=0),
    )(window_start, timestep, own, across, *beside, queries)


def body(main_qkv, guide_qkv, main_head, guide_head, window_start, timestep):
    groups = lax.axis_size("grp")
    tok = main_qkv.shape[0]
    heads = main_head.shape[0] // HD
    half = main_head.shape[1]
    assert groups * tok == TILE and window_start.shape[0] == lax.axis_size("seq")
    main = main_qkv.transpose(1, 0, 2)
    guide = guide_qkv.transpose(1, 0, 2)

    packed = pack_queries(main, guide, groups, heads)
    gathered = swapped(pack_keys(main, guide, guide_head.T, groups, heads))
    own = project_values(gathered, main_head.T, heads, tok, packed)
    across = traded(own, "seq", 1)
    beside = [traded(part, "seq", 0) for part in cut(own, (0, 4 * tok, own.shape[1] - 2 * tok, own.shape[1]))]
    queries = swapped(packed)
    part = attention(window_start, timestep, own, across, beside, queries, heads, tok, half)
    return jnp.sum(swapped(part).astype(jnp.float32), axis=0).T


def solution(mesh):
    in_specs = (
        P(("seq", "grp"), None, None),
        P(("seq", "grp"), None, None),
        P("grp", None),
        P(),
        P(),
        P(),
    )
    out_specs = P(("seq", "grp"), None)
    return jax.shard_map(body, mesh=mesh, in_specs=in_specs, out_specs=out_specs, check_vma=False)
```
